32 devices in a mesh: vol: 4 (over x, core), surf: 8 (over z, y).
Axes of the slice: x: 2, y: 2, z: 4, core: 2. Of those that a mesh axis runs over, the one named last changes fastest.
Arguments:
- points: float32 [3, 4096], P(None, ('vol', 'surf')), may hold values from -1 to 1
- surface_points: float32 [3, 8192], P(None, 'surf'), may hold values from -1 to 1
- displacement: float32 [3, 8192], P(None, 'surf'), may hold values from -6 to 6
- rotation: float32 [3, 8192], P(None, 'surf'), may hold values from -3 to 3
- halo_index: int32 [1024], P(('vol', 'surf')), may hold values from 0 to 127
- connectivity: int32 [4, 16384], P(None, ('vol', 'surf')), may hold values from 0 to 191
Outputs:
- node_motion: float32 [3, 4096], P(None, ('vol', 'surf'))
- swept: float32 [16384], P(('vol', 'surf'))
The draws below stay inside these ranges and needn't reach their ends.
All inputs are finite; a program needn't handle non-finite values.
Results may differ from the reference program's by a relative error of at most 0.0003.
Values sent between devices are 32-bit elements; how exact they have to be, the bound alone decides.
A program may use at most 64 MiB of HBM per device.

```python
import math
import jax
import jax.numpy as jnp
from jax import lax

VOL_DEV = 128
H_DEV = 32
CELLS_DEV = 512
NV = 4096
NS = 8192
NH = 1024
NC = 16384
DEVICES = 32


def with_ends(result, key, low, largest):
    longest = result.shape.index(max(result.shape))
    spots = []
    for shift in (0, 1):
        where = [jax.random.randint(jax.random.fold_in(key, axis), (), 0, length) for axis, length in enumerate(result.shape)]
        where[longest] = (where[longest] + shift) % result.shape[longest]
        spots.append(tuple(where))
    return result.at[spots[0]].set(low).at[spots[1]].set(largest)


def levels(stream_key, shape, shards, low, largest):
    factor_of = 1.0
    for axis_at, blocks in shards:
        steps = jax.random.uniform(jax.random.fold_in(jax.random.fold_in(stream_key, 6), axis_at), (blocks,), jnp.float32, low / len(shards), largest / len(shards))
        factor_of = factor_of * jnp.repeat(jnp.exp(steps), shape[axis_at] // blocks).reshape((-1,) + (1,) * (len(shape) - 1 - axis_at))
    return factor_of


def centred(key, dims, deviation, most, cuts=(), kind=jnp.bfloat16):
    array = jax.random.normal(key, dims, jnp.float32) * deviation
    if len(cuts) > 0:
        array = levels(key, dims, cuts, -0.22, 0.18) * array
    return jnp.clip(array, min=-most, max=most).astype(kind)


def setup_inputs(seed: int = 0) -> dict:
    splits = jax.random.split(jax.random.key(seed), 7)
    points = jnp.clip(jax.random.uniform(splits[0], (3, NV), jnp.float32, -1.0, 1.0) * levels(splits[0], (3, NV), ((1, 32),), -0.4, 0.0), -1.0, 1.0)
    surface_points = jnp.clip(jax.random.uniform(splits[1], (3, NS), jnp.float32, -1.0, 1.0) * levels(splits[1], (3, NS), ((1, 8),), -0.4, 0.0), -1.0, 1.0)
    displacement = centred(splits[2], (3, NS), 1.0, 6.0, ((1, 8),), jnp.float32)
    rotation = centred(splits[3], (3, NS), 0.5, 3.0, ((1, 8),), jnp.float32)
    halo_index = with_ends(jax.random.randint(splits[4], (NH,), 0, VOL_DEV), jax.random.fold_in(splits[4], 1), 0, VOL_DEV - 1).astype(jnp.int32)
    connectivity = with_ends(jax.random.randint(splits[5], (4, NC), 0, VOL_DEV + 2 * H_DEV), jax.random.fold_in(splits[5], 1), 0, (VOL_DEV + 2 * H_DEV) - 1).astype(jnp.int32)
    return dict(points=points, surface_points=surface_points, displacement=displacement, rotation=rotation, halo_index=halo_index, connectivity=connectivity)


SOFTENING = 0.01

def surface_terms(surface_points, displacement, rotation):
    rotated = jnp.cross(rotation, surface_points, axis=0)
    unit_row = jnp.ones_like(surface_points[0:1])
    return jnp.concatenate([displacement - rotated, rotation, unit_row], axis=0)

def pair_weight(node_points, anchors):
    gap_x = node_points[0][:, None] - anchors[0][None, :]
    gap_y = node_points[1][:, None] - anchors[1][None, :]
    gap_z = node_points[2][:, None] - anchors[2][None, :]
    spread = gap_x * gap_x + gap_y * gap_y + gap_z * gap_z + SOFTENING
    return lax.rsqrt(spread) / spread

def weighted_sums(node_points, anchors, term_rows):
    weight = pair_weight(node_points, anchors)
    return jnp.einsum('ns,cs->cn', weight, term_rows, precision=lax.Precision.HIGHEST)

def node_shift(node_points, totals):
    return (totals[0:3] + jnp.cross(totals[3:6], node_points, axis=0)) / totals[6:7]

def swept_volume(corners):
    initial = corners[0:3]
    motion = corners[3:6]
    halfway = initial + 0.5 * motion
    face_list = ((1, 2, 3), (0, 3, 2), (0, 1, 3), (0, 2, 1))
    swept_sum = jnp.zeros(corners.shape[2:], corners.dtype)
    for first, second, third in face_list:
        normal = 0.5 * jnp.cross(halfway[:, second] - halfway[:, first], halfway[:, third] - halfway[:, first], axis=0)
        average = (motion[:, first] + motion[:, second] + motion[:, third]) / 3.0
        swept_sum = swept_sum + lax.optimization_barrier(jnp.sum(average * normal, axis=0))
    return swept_sum

def reference(points, surface_points, displacement, rotation, halo_index, connectivity):
    term_rows = surface_terms(surface_points, displacement, rotation)
    block_size = math.gcd(NV, 512)
    block_count = NV // block_size
    blocks = points.reshape(3, block_count, block_size).transpose(1, 0, 2)
    totals = lax.map(lambda block_points: weighted_sums(block_points, surface_points, term_rows), blocks)
    totals = totals.transpose(1, 0, 2).reshape(7, NV)
    node_motion = node_shift(points, totals)
    node_state = jnp.concatenate([points, node_motion], axis=0).reshape(6, DEVICES, VOL_DEV)
    rim_index = halo_index.reshape(DEVICES, H_DEV).astype(jnp.int32)
    lent = jnp.take_along_axis(node_state, rim_index[None], axis=2)
    extended = jnp.concatenate([jnp.roll(lent, 1, axis=1), node_state, jnp.roll(lent, -1, axis=1)], axis=2)
    cell_nodes = connectivity.reshape(4, DEVICES, CELLS_DEV).astype(jnp.int32)

    def pick_corners(block_state, block_cells):
        return block_state[:, block_cells]
    corners = jax.vmap(pick_corners, in_axes=(1, 1), out_axes=2)(extended, cell_nodes)
    swept = swept_volume(corners).reshape(NC)
    return (node_motion, swept)
```

```python
import functools

import jax
import jax.numpy as jnp
from jax import lax
from jax.experimental import pallas as pl
from jax.experimental.pallas import tpu as pltpu
from jax.sharding import PartitionSpec as P

SOFTENING = 0.01
LANES = 128
ROWS = 8
CHUNK = 256
STEP = 32
FACES = ((1, 2, 3), (0, 3, 2), (0, 1, 3), (0, 2, 1))
MESH = pl.DeviceIdType.MESH


def cross(a, b):
    return (
        a[1] * b[2] - a[2] * b[1],
        a[2] * b[0] - a[0] * b[2],
        a[0] * b[1] - a[1] * b[0],
    )


def split_rows(rows):
    first = rows.astype(jnp.bfloat16)
    rest = rows - first.astype(jnp.float32)
    second = rest.astype(jnp.bfloat16)
    third = rest - second.astype(jnp.float32)
    return jnp.concatenate(
        [first.astype(jnp.float32), second.astype(jnp.float32), third, jnp.zeros_like(rows)], axis=0
    ).astype(jnp.bfloat16)


def pick(rows, index):
    return jnp.take_along_axis(rows, index, axis=1)


def node_shift(totals, rows):
    turn = cross((totals[3:4], totals[4:5], totals[5:6]), (rows[0:1], rows[1:2], rows[2:3]))
    scale = 1.0 / totals[6:7]
    return tuple((totals[k : k + 1] + turn[k]) * scale for k in range(3))


def kernel(
    tiles,
    parts,
    width,
    points_ref,
    surface_ref,
    displacement_ref,
    rotation_ref,
    halo_ref,
    cells_ref,
    motion_ref,
    swept_ref,
    nodes,
    anchors,
    terms,
    high,
    low,
    partial,
    lent,
    got_own,
    got_lent,
    got_far,
    send_sems,
    recv_sems,
):
    tile = lax.axis_index("vol")
    me = lax.axis_index("surf")
    before = lax.rem(tile + tiles - 1, tiles)
    after = lax.rem(tile + 1, tiles)
    is_first = me == 0
    is_last = me == parts - 1

    def bulk(ref, count, sem):
        return pltpu.make_async_copy(ref.at[pl.ds(0, count)], ref.at[pl.ds(0, count)], sem)

    def remote(src, dst, kind, device):
        return pltpu.make_async_remote_copy(
            src_ref=src,
            dst_ref=dst,
            send_sem=send_sems.at[kind],
            recv_sem=recv_sems.at[kind],
            device_id=device,
            device_id_type=MESH,
        )

    barrier = pltpu.get_barrier_semaphore()

    def greet(other, _):
        @pl.when(other != me)
        def _():
            pl.semaphore_signal(barrier, inc=1, device_id=(tile, other), device_id_type=MESH)

        @pl.when(is_first)
        def _():
            pl.semaphore_signal(barrier, inc=1, device_id=(before, other), device_id_type=MESH)

        @pl.when(is_last)
        def _():
            pl.semaphore_signal(barrier, inc=1, device_id=(after, other), device_id_type=MESH)

        return 0

    lax.fori_loop(0, parts, greet, 0)

    halo = halo_ref[...].astype(jnp.float32)
    halo_row = jnp.concatenate([halo] * (LANES // width), axis=1)
    mine = jnp.concatenate(
        [points_ref[...], halo_row, jnp.zeros((ROWS - 4, LANES), jnp.float32)], axis=0
    )
    nodes[me] = mine
    pl.semaphore_wait(barrier, parts + 1)

    def share(step, _):
        other = lax.rem(me + step, parts)
        remote(nodes.at[me], nodes.at[me], 0, (tile, other)).start()
        return 0

    lax.fori_loop(1, parts, share, 0)

    @pl.when(is_last)
    def _():
        remote(nodes.at[me], nodes.at[parts], 1, (after, 0)).start()

    @pl.when(is_first)
    def _():
        remote(nodes.at[me], nodes.at[parts + 1], 1, (before, parts - 1)).start()

    depth = surface_ref.shape[1]
    surface = surface_ref[...]
    rotation = rotation_ref[...]
    turned = cross(
        tuple(rotation[k : k + 1] for k in range(3)), tuple(surface[k : k + 1] for k in range(3))
    )
    rows = jnp.concatenate(
        [
            displacement_ref[...] - jnp.concatenate(turned, axis=0),
            rotation,
            jnp.ones((1, depth), jnp.float32),
            jnp.zeros((1, depth), jnp.float32),
        ],
        axis=0,
    )
    terms[...] = split_rows(rows)
    padded = jnp.concatenate([surface, jnp.zeros((ROWS - 3, depth), jnp.float32)], axis=0)
    for start in range(0, depth, LANES):
        upright = padded[:, start : start + LANES].T
        for k in range(3):
            anchors[k, start : start + LANES] = jnp.broadcast_to(
                upright[:, k : k + 1], (LANES, LANES)
            )

    groups = cells_ref.shape[1] // LANES
    corner = jnp.concatenate(
        [
            cells_ref[k : k + 1, g * LANES : (g + 1) * LANES]
            for k in range(4)
            for g in range(groups)
        ],
        axis=0,
    )
    is_own = (corner >= width) & (corner < width + LANES)
    own_at = jnp.where(is_own, corner - width, 0)
    lent_at = jnp.where(is_own, 0, jnp.where(corner < width, corner, corner - LANES))

    def corners(own_row, lent_row):
        found = []
        for r in range(0, 4 * groups, ROWS):
            cut = slice(r, r + ROWS)
            found.append(
                jnp.where(
                    is_own[cut],
                    pick(jnp.broadcast_to(own_row, (ROWS, LANES)), own_at[cut]),
                    pick(jnp.broadcast_to(lent_row, (ROWS, LANES)), lent_at[cut]),
                )
            )
        whole = jnp.concatenate(found, axis=0)
        return [whole[k * groups : (k + 1) * groups] for k in range(4)]

    bulk(nodes, parts - 1, recv_sems.at[0]).wait()

    pair = 2 if parts % 2 == 0 else 1

    def sums(step, _):
        base = lax.rem(me // pair + 1 + step, parts // pair) * pair
        places = [nodes[base + k] for k in range(pair)]
        total = jnp.zeros((4 * ROWS, pair * LANES), jnp.float32)
        for start in range(0, depth, CHUNK):
            for row in range(start, start + CHUNK, STEP):
                cut = slice(row, row + STEP)
                sx, sy, sz = anchors[0, cut], anchors[1, cut], anchors[2, cut]
                for k in range(pair):
                    gx = sx - places[k][0:1]
                    gy = sy - places[k][1:2]
                    gz = sz - places[k][2:3]
                    root = lax.rsqrt(gx * gx + gy * gy + (gz * gz + SOFTENING))
                    weight = root * root * root
                    top = weight.astype(jnp.bfloat16)
                    side = slice(k * LANES, (k + 1) * LANES)
                    high[cut, side] = top
                    low[cut, side] = (weight - top.astype(jnp.float32)).astype(jnp.bfloat16)
            cut = slice(start, start + CHUNK)
            left = terms[:, cut]
            total = total + jnp.dot(left, high[cut], preferred_element_type=jnp.float32)
            total = total + jnp.dot(left, low[cut], preferred_element_type=jnp.float32)
        added = total[0:ROWS] + total[ROWS : 2 * ROWS] + total[2 * ROWS : 3 * ROWS]
        for k in range(pair):
            block = base + k
            partial[block] = added[:, k * LANES : (k + 1) * LANES]

            @pl.when(block != me)
            def _():
                remote(partial.at[block], got_own.at[me], 2, (tile, block)).start()

        return 0

    lax.fori_loop(0, parts // pair, sums, 0)
    got_own[me] = partial[me]

    lane = lax.broadcasted_iota(jnp.int32, (ROWS, LANES), 1)
    is_before = lane < width

    def lent_of(values, slot):
        index = jnp.broadcast_to(nodes[slot][3:4], (ROWS, LANES)).astype(jnp.int32)
        return pick(values, index)

    def lend(step, _):
        block = lax.rem(me + 1 + step, parts)
        low_side = jnp.maximum(block - 1, 0)
        high_side = jnp.minimum(block + 1, parts - 1)
        first = lent_of(partial[low_side], low_side) * jnp.where(block > 0, 1.0, 0.0)
        second = lent_of(partial[high_side], high_side) * jnp.where(block < parts - 1, 1.0, 0.0)
        lent[block] = jnp.where(is_before, first, second)

        @pl.when(block != me)
        def _():
            remote(lent.at[block], got_lent.at[me], 3, (tile, block)).start()

        return 0

    lent[parts] = jnp.where(is_before, lent_of(partial[parts - 1], parts - 1), 0.0)
    remote(lent.at[parts], got_far.at[me], 4, (after, 0)).start()
    lent[parts + 1] = jnp.where(is_before, 0.0, lent_of(partial[0], 0))
    remote(lent.at[parts + 1], got_far.at[me], 4, (before, parts - 1)).start()
    lax.fori_loop(0, parts, lend, 0)
    got_lent[me] = lent[me]

    @pl.when(is_first)
    def _():
        bulk(nodes, 1, recv_sems.at[1]).wait()

    @pl.when(is_last)
    def _():
        bulk(nodes, 1, recv_sems.at[1]).wait()

    slot_before = jnp.where(is_first, parts, me - 1)
    slot_after = jnp.where(is_last, parts + 1, me + 1)
    lent_nodes = jnp.where(
        is_before,
        lent_of(nodes[slot_before], slot_before),
        lent_of(nodes[slot_after], slot_after),
    )
    place = [corners(mine[k : k + 1], lent_nodes[k : k + 1]) for k in range(3)]

    bulk(got_own, parts - 1, recv_sems.at[2]).wait()
    own_totals = jnp.sum(got_own[...], axis=0)
    own_motion = node_shift(own_totals, mine)
    motion_ref[...] = jnp.concatenate(own_motion, axis=0)

    @pl.when(jnp.logical_not(is_first | is_last))
    def _():
        got_far[...] = jnp.zeros_like(got_far)

    bulk(got_lent, parts - 1, recv_sems.at[3]).wait()

    @pl.when(is_first | is_last)
    def _():
        bulk(got_far, parts, recv_sems.at[4]).wait()

    lent_totals = jnp.sum(got_lent[...] + got_far[...], axis=0)
    lent_motion = node_shift(lent_totals, lent_nodes)
    shift = [corners(own_motion[k], lent_motion[k]) for k in range(3)]

    half = [[place[k][c] + 0.5 * shift[k][c] for c in range(4)] for k in range(3)]
    swept = jnp.zeros((groups, LANES), jnp.float32)
    for first, second, third in FACES:
        normal = cross(
            [half[k][second] - half[k][first] for k in range(3)],
            [half[k][third] - half[k][first] for k in range(3)],
        )
        for k in range(3):
            swept = swept + (shift[k][first] + shift[k][second] + shift[k][third]) * normal[k]
    swept_ref[...] = swept * (1.0 / 6.0)

    bulk(nodes, parts - 1, send_sems.at[0]).wait()

    @pl.when(is_first)
    def _():
        bulk(nodes, 1, send_sems.at[1]).wait()

    @pl.when(is_last)
    def _():
        bulk(nodes, 1, send_sems.at[1]).wait()

    bulk(partial, parts - 1, send_sems.at[2]).wait()
    bulk(lent, parts - 1, send_sems.at[3]).wait()
    bulk(lent, 2, send_sems.at[4]).wait()


def shards(tiles, parts, points, surface_points, displacement, rotation, halo_index, connectivity):
    width = halo_index.shape[0]
    depth = surface_points.shape[1]
    cells = connectivity.shape[1]
    pair = 2 if parts % 2 == 0 else 1
    block = (ROWS, LANES)
    motion, swept = pl.pallas_call(
        functools.partial(kernel, tiles, parts, width),
        out_shape=(
            jax.ShapeDtypeStruct((3, LANES), jnp.float32),
            jax.ShapeDtypeStruct((cells // LANES, LANES), jnp.float32),
        ),
        in_specs=[pl.BlockSpec(memory_space=pltpu.VMEM)] * 6,
        out_specs=(pl.BlockSpec(memory_space=pltpu.VMEM),) * 2,
        scratch_shapes=[
            pltpu.VMEM((parts + 2, *block), jnp.float32),
            pltpu.VMEM((3, depth, LANES), jnp.float32),
            pltpu.VMEM((4 * ROWS, depth), jnp.bfloat16),
            pltpu.VMEM((depth, pair * LANES), jnp.bfloat16),
            pltpu.VMEM((depth, pair * LANES), jnp.bfloat16),
            pltpu.VMEM((parts, *block), jnp.float32),
            pltpu.VMEM((parts + 2, *block), jnp.float32),
            pltpu.VMEM((parts, *block), jnp.float32),
            pltpu.VMEM((parts, *block), jnp.float32),
            pltpu.VMEM((parts, *block), jnp.float32),
            pltpu.SemaphoreType.DMA((5,)),
            pltpu.SemaphoreType.DMA((5,)),
        ],
        compiler_params=pltpu.CompilerParams(
            collective_id=0, has_side_effects=True, vmem_limit_bytes=16 * 1024 * 1024
        ),
        cost_estimate=pl.CostEstimate(
            flops=2 * 7 * parts * LANES * depth,
            bytes_accessed=4 * (9 * depth + 4 * cells),
            transcendentals=parts * LANES * depth,
        ),
    )(points, surface_points, displacement, rotation, halo_index.reshape(1, width), connectivity)
    return motion, swept.reshape(cells)


def solution(mesh):
    in_specs = (
        P(None, ("vol", "surf")),
        P(None, "surf"),
        P(None, "surf"),
        P(None, "surf"),
        P(("vol", "surf")),
        P(None, ("vol", "surf")),
    )
    out_specs = (P(None, ("vol", "surf")), P(("vol", "surf")))
    body = functools.partial(shards, mesh.shape["vol"], mesh.shape["surf"])
    return jax.shard_map(body, mesh=mesh, in_specs=in_specs, out_specs=out_specs, check_vma=False)
```

```python
import functools

import jax
import jax.numpy as jnp
from jax import lax
from jax.experimental import pallas as pl
from jax.experimental.pallas import tpu as pltpu
from jax.sharding import PartitionSpec as P

SOFTENING = 0.01
LANES = 128
ROWS = 8
CHUNK = 256
STEP = 32
FACES = ((1, 2, 3), (0, 3, 2), (0, 1, 3), (0, 2, 1))
MESH = pl.DeviceIdType.MESH


def cross(a, b):
    return (
        a[1] * b[2] - a[2] * b[1],
        a[2] * b[0] - a[0] * b[2],
        a[0] * b[1] - a[1] * b[0],
    )


def split_rows(rows):
    first = rows.astype(jnp.bfloat16)
    rest = rows - first.astype(jnp.float32)
    second = rest.astype(jnp.bfloat16)
    third = rest - second.astype(jnp.float32)
    return jnp.concatenate(
        [first.astype(jnp.float32), second.astype(jnp.float32), third, jnp.zeros_like(rows)], axis=0
    ).astype(jnp.bfloat16)


def pick(rows, index):
    return jnp.take_along_axis(rows, index, axis=1)


def node_shift(totals, rows):
    turn = cross((totals[3:4], totals[4:5], totals[5:6]), (rows[0:1], rows[1:2], rows[2:3]))
    scale = 1.0 / totals[6:7]
    return tuple((totals[k : k + 1] + turn[k]) * scale for k in range(3))


def kernel(
    tiles,
    parts,
    width,
    points_in,
    surface_in,
    displacement_in,
    rotation_in,
    halo_in,
    cells_in,
    result_ref,
    points_ref,
    surface_ref,
    displacement_ref,
    rotation_ref,
    halo_ref,
    cells_ref,
    nodes,
    anchors,
    terms,
    high,
    low,
    partial,
    lent,
    got_own,
    got_before,
    got_after,
    load_sems,
    node_send_sems,
    node_recv_sems,
    send_sems,
    recv_sems,
):
    tile = lax.axis_index("vol")
    me = lax.axis_index("surf")
    before = lax.rem(tile + tiles - 1, tiles)
    after = lax.rem(tile + 1, tiles)
    is_first = me == 0
    is_last = me == parts - 1

    sources = (points_in, halo_in, surface_in, rotation_in, displacement_in, cells_in)
    targets = (points_ref, halo_ref, surface_ref, rotation_ref, displacement_ref, cells_ref)
    loads = [
        pltpu.make_async_copy(source, target, load_sems.at[k])
        for k, (source, target) in enumerate(zip(sources, targets))
    ]
    for load in loads:
        load.start()

    def bulk(ref, count, sem):
        return pltpu.make_async_copy(ref.at[pl.ds(0, count)], ref.at[pl.ds(0, count)], sem)

    def remote(src, dst, send_sem, recv_sem, device):
        return pltpu.make_async_remote_copy(
            src_ref=src,
            dst_ref=dst,
            send_sem=send_sem,
            recv_sem=recv_sem,
            device_id=device,
            device_id_type=MESH,
        )

    barrier = pltpu.get_barrier_semaphore()

    def greet(step, _):
        other = lax.rem(me + step, parts)
        pl.semaphore_signal(barrier, inc=1, device_id=(tile, other), device_id_type=MESH)
        return 0

    def greet_far(far):
        def body(other, _):
            pl.semaphore_signal(barrier, inc=1, device_id=(far, other), device_id_type=MESH)
            return 0

        lax.fori_loop(0, parts, body, 0)

    lax.fori_loop(1, parts, greet, 0)

    @pl.when(is_first)
    def _():
        greet_far(before)

    @pl.when(is_last)
    def _():
        greet_far(after)

    loads[0].wait()
    loads[1].wait()
    halo = halo_ref[...].astype(jnp.float32)
    halo_row = jnp.concatenate([halo] * (LANES // width), axis=1)
    mine = jnp.concatenate(
        [points_ref[...], halo_row, jnp.zeros((ROWS - 4, LANES), jnp.float32)], axis=0
    )
    nodes[me] = mine
    pl.semaphore_wait(barrier, parts + 1)

    def share(step, _):
        other = lax.rem(me + step, parts)
        remote(
            nodes.at[me], nodes.at[me], node_send_sems.at[0], node_recv_sems.at[me], (tile, other)
        ).start()
        return 0

    lax.fori_loop(1, parts, share, 0)

    def share_far(slot, device):
        remote(
            nodes.at[me], nodes.at[slot], node_send_sems.at[1], node_recv_sems.at[slot], device
        ).start()

    @pl.when(is_last)
    def _():
        share_far(parts, (after, 0))

    @pl.when(is_first)
    def _():
        share_far(parts + 1, (before, parts - 1))

    for load in loads[2:5]:
        load.wait()
    depth = surface_ref.shape[1]
    surface = surface_ref[...]
    rotation = rotation_ref[...]
    turned = cross(
        tuple(rotation[k : k + 1] for k in range(3)), tuple(surface[k : k + 1] for k in range(3))
    )
    rows = jnp.concatenate(
        [
            displacement_ref[...] - jnp.concatenate(turned, axis=0),
            rotation,
            jnp.ones((1, depth), jnp.float32),
            jnp.zeros((1, depth), jnp.float32),
        ],
        axis=0,
    )
    terms[...] = split_rows(rows)
    padded = jnp.concatenate([surface, jnp.zeros((ROWS - 3, depth), jnp.float32)], axis=0)
    for start in range(0, depth, LANES):
        upright = padded[:, start : start + LANES].T
        for k in range(3):
            anchors[k, start : start + LANES] = jnp.broadcast_to(
                upright[:, k : k + 1], (LANES, LANES)
            )

    def lent_of(values, slot):
        index = jnp.broadcast_to(nodes[slot][3:4], (ROWS, LANES)).astype(jnp.int32)
        return pick(values, index)

    pair = 2 if parts % 2 == 0 else 1
    pairs = parts // pair
    turn = 1 - 2 * jnp.minimum((me // pair) // max(pairs // 2, 1), 1)

    def sums(step, _):
        base = lax.rem(me // pair + turn * step + pairs, pairs) * pair
        for k in range(pair):

            @pl.when(base + k != me)
            def _():
                pltpu.make_async_copy(
                    nodes.at[base + k], nodes.at[base + k], node_recv_sems.at[base + k]
                ).wait()

        places = [nodes[base + k] for k in range(pair)]
        total = jnp.zeros((4 * ROWS, pair * LANES), jnp.float32)
        for start in range(0, depth, CHUNK):
            for row in range(start, start + CHUNK, STEP):
                cut = slice(row, row + STEP)
                sx, sy, sz = anchors[0, cut], anchors[1, cut], anchors[2, cut]
                for k in range(pair):
                    gx = sx - places[k][0:1]
                    gy = sy - places[k][1:2]
                    gz = sz - places[k][2:3]
                    root = lax.rsqrt(gx * gx + gy * gy + (gz * gz + SOFTENING))
                    weight = root * root * root
                    top = weight.astype(jnp.bfloat16)
                    side = slice(k * LANES, (k + 1) * LANES)
                    high[cut, side] = top
                    low[cut, side] = (weight - top.astype(jnp.float32)).astype(jnp.bfloat16)
            cut = slice(start, start + CHUNK)
            left = terms[:, cut]
            total = total + jnp.dot(left, high[cut], preferred_element_type=jnp.float32)
            total = total + jnp.dot(left, low[cut], preferred_element_type=jnp.float32)
        added = total[0:ROWS] + total[ROWS : 2 * ROWS] + total[2 * ROWS : 3 * ROWS]
        halves = [added[:, k * LANES : (k + 1) * LANES] for k in range(pair)]
        for k in range(pair):
            partial[base + k] = halves[k]
        for k in range(pair):
            lent[base + k] = lent_of(halves[k], base + k)
        for k in range(pair):
            block = base + k
            is_mine = block == me

            @pl.when(is_mine)
            def _():
                got_own[me] = halves[k]

            @pl.when(jnp.logical_not(is_mine))
            def _():
                remote(
                    partial.at[block], got_own.at[me], send_sems.at[0], recv_sems.at[0], (tile, block)
                ).start()

            is_end = block == parts - 1
            owner = (jnp.where(is_end, after, tile), jnp.where(is_end, 0, block + 1))

            @pl.when(block + 1 == me)
            def _():
                got_before[me] = lent[block]

            @pl.when(block + 1 != me)
            def _():
                remote(
                    lent.at[block], got_before.at[me], send_sems.at[1], recv_sems.at[1], owner
                ).start()

            is_start = block == 0
            other = (jnp.where(is_start, before, tile), jnp.where(is_start, parts - 1, block - 1))

            @pl.when(block - 1 == me)
            def _():
                got_after[me] = lent[block]

            @pl.when(block - 1 != me)
            def _():
                remote(
                    lent.at[block], got_after.at[me], send_sems.at[2], recv_sems.at[2], other
                ).start()

        return 0

    lax.fori_loop(0, pairs, sums, 0)

    loads[5].wait()
    groups = cells_ref.shape[1] // LANES
    corner = jnp.concatenate(
        [
            cells_ref[k : k + 1, g * LANES : (g + 1) * LANES]
            for k in range(4)
            for g in range(groups)
        ],
        axis=0,
    )
    is_own = (corner >= width) & (corner < width + LANES)
    own_at = jnp.where(is_own, corner - width, 0)
    lent_at = jnp.where(is_own, 0, jnp.where(corner < width, corner, corner - LANES))

    def corners(own_row, lent_row):
        found = []
        for r in range(0, 4 * groups, ROWS):
            cut = slice(r, r + ROWS)
            found.append(
                jnp.where(
                    is_own[cut],
                    pick(jnp.broadcast_to(own_row, (ROWS, LANES)), own_at[cut]),
                    pick(jnp.broadcast_to(lent_row, (ROWS, LANES)), lent_at[cut]),
                )
            )
        whole = jnp.concatenate(found, axis=0)
        return [whole[k * groups : (k + 1) * groups] for k in range(4)]

    lane = lax.broadcasted_iota(jnp.int32, (ROWS, LANES), 1)
    is_before = lane < width

    @pl.when(is_first)
    def _():
        pltpu.make_async_copy(nodes.at[parts], nodes.at[parts], node_recv_sems.at[parts]).wait()

    @pl.when(is_last)
    def _():
        pltpu.make_async_copy(
            nodes.at[parts + 1], nodes.at[parts + 1], node_recv_sems.at[parts + 1]
        ).wait()

    slot_before = jnp.where(is_first, parts, me - 1)
    slot_after = jnp.where(is_last, parts + 1, me + 1)
    lent_nodes = jnp.where(
        is_before,
        lent_of(nodes[slot_before], slot_before),
        lent_of(nodes[slot_after], slot_after),
    )
    place = [corners(mine[k : k + 1], lent_nodes[k : k + 1]) for k in range(3)]

    bulk(got_own, parts - 1, recv_sems.at[0]).wait()
    own_totals = jnp.sum(got_own[...], axis=0)
    own_motion = node_shift(own_totals, mine)

    def wait_side(ref, is_edge, sem):
        @pl.when(is_edge)
        def _():
            bulk(ref, parts, sem).wait()

        @pl.when(jnp.logical_not(is_edge))
        def _():
            bulk(ref, parts - 1, sem).wait()

    wait_side(got_before, is_first, recv_sems.at[1])
    wait_side(got_after, is_last, recv_sems.at[2])
    lent_totals = jnp.where(
        is_before, jnp.sum(got_before[...], axis=0), jnp.sum(got_after[...], axis=0)
    )
    lent_motion = node_shift(lent_totals, lent_nodes)
    shift = [corners(own_motion[k], lent_motion[k]) for k in range(3)]

    half = [[place[k][c] + 0.5 * shift[k][c] for c in range(4)] for k in range(3)]
    swept = jnp.zeros((groups, LANES), jnp.float32)
    for first, second, third in FACES:
        normal = cross(
            [half[k][second] - half[k][first] for k in range(3)],
            [half[k][third] - half[k][first] for k in range(3)],
        )
        for k in range(3):
            swept = swept + (shift[k][first] + shift[k][second] + shift[k][third]) * normal[k]
    result_ref[0:3] = jnp.concatenate(own_motion, axis=0)
    result_ref[3 : 3 + groups] = swept * (1.0 / 6.0)

    bulk(nodes, parts - 1, node_send_sems.at[0]).wait()

    @pl.when(is_first)
    def _():
        bulk(nodes, 1, node_send_sems.at[1]).wait()

    @pl.when(is_last)
    def _():
        bulk(nodes, 1, node_send_sems.at[1]).wait()

    bulk(partial, parts - 1, send_sems.at[0]).wait()
    wait_side(lent, is_first, send_sems.at[1])
    wait_side(lent, is_last, send_sems.at[2])


def part_kernel(groups, result_ref, motion_ref, swept_ref):
    motion_ref[...] = result_ref[0:3]
    swept_ref[...] = result_ref[3 : 3 + groups]


def shards(tiles, parts, points, surface_points, displacement, rotation, halo_index, connectivity):
    width = halo_index.shape[0]
    depth = surface_points.shape[1]
    cells = connectivity.shape[1]
    groups = cells // LANES
    pair = 2 if parts % 2 == 0 else 1
    block = (ROWS, LANES)
    dma = pltpu.SemaphoreType.DMA
    result = pl.pallas_call(
        functools.partial(kernel, tiles, parts, width),
        out_shape=jax.ShapeDtypeStruct((-(-(3 + groups) // ROWS) * ROWS, LANES), jnp.float32),
        in_specs=[pl.BlockSpec(memory_space=pltpu.HBM)] * 6,
        out_specs=pl.BlockSpec(memory_space=pltpu.VMEM),
        scratch_shapes=[
            pltpu.VMEM((3, LANES), jnp.float32),
            pltpu.VMEM((3, depth), jnp.float32),
            pltpu.VMEM((3, depth), jnp.float32),
            pltpu.VMEM((3, depth), jnp.float32),
            pltpu.VMEM((1, width), jnp.int32),
            pltpu.VMEM((4, cells), jnp.int32),
            pltpu.VMEM((parts + 2, *block), jnp.float32),
            pltpu.VMEM((3, depth, LANES), jnp.float32),
            pltpu.VMEM((4 * ROWS, depth), jnp.bfloat16),
            pltpu.VMEM((depth, pair * LANES), jnp.bfloat16),
            pltpu.VMEM((depth, pair * LANES), jnp.bfloat16),
            pltpu.VMEM((parts, *block), jnp.float32),
            pltpu.VMEM((parts, *block), jnp.float32),
            pltpu.VMEM((parts, *block), jnp.float32),
            pltpu.VMEM((parts, *block), jnp.float32),
            pltpu.VMEM((parts, *block), jnp.float32),
            dma((6,)),
            dma((2,)),
            dma((parts + 2,)),
            dma((3,)),
            dma((3,)),
        ],
        compiler_params=pltpu.CompilerParams(
            collective_id=0, has_side_effects=True, vmem_limit_bytes=60 * 1024 * 1024
        ),
        cost_estimate=pl.CostEstimate(
            flops=2 * 7 * parts * LANES * depth,
            bytes_accessed=4 * (9 * depth + 4 * cells),
            transcendentals=parts * LANES * depth,
        ),
    )(points, surface_points, displacement, rotation, halo_index.reshape(1, width), connectivity)
    motion, swept = pl.pallas_call(
        functools.partial(part_kernel, groups),
        out_shape=(
            jax.ShapeDtypeStruct((3, LANES), jnp.float32),
            jax.ShapeDtypeStruct((groups, LANES), jnp.float32),
        ),
        in_specs=[pl.BlockSpec(memory_space=pltpu.VMEM)],
    )(result)
    return motion, swept.reshape(cells)


def solution(mesh):
    in_specs = (
        P(None, ("vol", "surf")),
        P(None, "surf"),
        P(None, "surf"),
        P(None, "surf"),
        P(("vol", "surf")),
        P(None, ("vol", "surf")),
    )
    out_specs = (P(None, ("vol", "surf")), P(("vol", "surf")))
    body = functools.partial(shards, mesh.shape["vol"], mesh.shape["surf"])
    return jax.shard_map(body, mesh=mesh, in_specs=in_specs, out_specs=out_specs, check_vma=False)
```

```python
import functools

import jax
import jax.numpy as jnp
from jax import lax
from jax.experimental import pallas as pl
from jax.experimental.pallas import tpu as pltpu
from jax.sharding import PartitionSpec as P

SOFTENING = 0.01
LANES = 128
ROWS = 8
CHUNK = 256
STEP = 64
FACES = ((1, 2, 3), (0, 3, 2), (0, 1, 3), (0, 2, 1))
MESH = pl.DeviceIdType.MESH


def cross(a, b):
    return (
        a[1] * b[2] - a[2] * b[1],
        a[2] * b[0] - a[0] * b[2],
        a[0] * b[1] - a[1] * b[0],
    )


def three_terms(rows):
    first = rows.astype(jnp.bfloat16).astype(jnp.float32)
    rest = rows - first
    second = rest.astype(jnp.bfloat16).astype(jnp.float32)
    return first, second, (rest - second).astype(jnp.bfloat16).astype(jnp.float32)


def stack(*blocks):
    return jnp.concatenate(blocks, axis=0)


def node_factors(rows):
    x, y, z = rows[0:1], rows[1:2], rows[2:3]
    ones = jnp.ones_like(x)
    first, second, third = three_terms(
        stack(-2.0 * x, -2.0 * y, -2.0 * z, x * x + y * y + z * z, ones, 0.0 * ones, 0.0 * ones, 0.0 * ones)
    )
    return stack(first, first, second, second, first, third)


def surface_factors(rows):
    x, y, z = rows[0:1], rows[1:2], rows[2:3]
    ones = jnp.ones_like(x)
    first, second, third = three_terms(
        stack(x, y, z, ones, x * x + y * y + (z * z + SOFTENING), 0.0 * ones, 0.0 * ones, 0.0 * ones)
    )
    return stack(first, second, first, second, third, first)


def pick(rows, index):
    return jnp.take_along_axis(rows, index, axis=1)


def node_shift(totals, rows):
    turn = cross((totals[3:4], totals[4:5], totals[5:6]), (rows[0:1], rows[1:2], rows[2:3]))
    scale = 1.0 / totals[6:7]
    return tuple((totals[k : k + 1] + turn[k]) * scale for k in range(3))


def kernel(
    tiles,
    parts,
    width,
    points_in,
    surface_in,
    displacement_in,
    rotation_in,
    halo_in,
    cells_in,
    motion_out,
    swept_out,
    points_ref,
    surface_ref,
    displacement_ref,
    rotation_ref,
    halo_ref,
    cells_ref,
    nodes,
    anchors,
    terms,
    high,
    low,
    partial,
    lent,
    got_own,
    got_before,
    got_after,
    motion_ref,
    swept_ref,
    load_sems,
    node_send_sems,
    node_recv_sems,
    send_sems,
    recv_sems,
):
    tile = lax.axis_index("vol")
    me = lax.axis_index("surf")
    before = lax.rem(tile + tiles - 1, tiles)
    after = lax.rem(tile + 1, tiles)
    is_first = me == 0
    is_last = me == parts - 1

    sources = (points_in, halo_in, surface_in, rotation_in, displacement_in, cells_in)
    targets = (points_ref, halo_ref, surface_ref, rotation_ref, displacement_ref, cells_ref)
    loads = [
        pltpu.make_async_copy(source, target, load_sems.at[k])
        for k, (source, target) in enumerate(zip(sources, targets))
    ]
    for load in loads:
        load.start()

    def bulk(ref, count, sem):
        return pltpu.make_async_copy(ref.at[pl.ds(0, count)], ref.at[pl.ds(0, count)], sem)

    def remote(src, dst, send_sem, recv_sem, device):
        return pltpu.make_async_remote_copy(
            src_ref=src,
            dst_ref=dst,
            send_sem=send_sem,
            recv_sem=recv_sem,
            device_id=device,
            device_id_type=MESH,
        )

    barrier = pltpu.get_barrier_semaphore()

    def greet(step, _):
        other = lax.rem(me + step, parts)
        pl.semaphore_signal(barrier, inc=1, device_id=(tile, other), device_id_type=MESH)
        return 0

    def greet_far(far):
        def body(other, _):
            pl.semaphore_signal(barrier, inc=1, device_id=(far, other), device_id_type=MESH)
            return 0

        lax.fori_loop(0, parts, body, 0)

    lax.fori_loop(1, parts, greet, 0)

    @pl.when(is_first)
    def _():
        greet_far(before)

    @pl.when(is_last)
    def _():
        greet_far(after)

    loads[0].wait()
    loads[1].wait()
    halo = halo_ref[...].astype(jnp.float32)
    halo_row = jnp.concatenate([halo] * (LANES // width), axis=1)
    mine = jnp.concatenate(
        [points_ref[...], halo_row, jnp.zeros((ROWS - 4, LANES), jnp.float32)], axis=0
    )
    nodes[me] = mine
    pl.semaphore_wait(barrier, parts + 1)

    def share(step, _):
        other = lax.rem(me + step, parts)
        remote(
            nodes.at[me], nodes.at[me], node_send_sems.at[0], node_recv_sems.at[me], (tile, other)
        ).start()
        return 0

    lax.fori_loop(1, parts, share, 0)

    def share_far(slot, device):
        remote(
            nodes.at[me], nodes.at[slot], node_send_sems.at[1], node_recv_sems.at[slot], device
        ).start()

    @pl.when(is_last)
    def _():
        share_far(parts, (after, 0))

    @pl.when(is_first)
    def _():
        share_far(parts + 1, (before, parts - 1))

    for load in loads[2:5]:
        load.wait()
    depth = surface_ref.shape[1]
    surface = surface_ref[...]
    rotation = rotation_ref[...]
    turned = cross(
        tuple(rotation[k : k + 1] for k in range(3)), tuple(surface[k : k + 1] for k in range(3))
    )
    rows = jnp.concatenate(
        [
            displacement_ref[...] - jnp.concatenate(turned, axis=0),
            rotation,
            jnp.ones((1, depth), jnp.float32),
            jnp.zeros((1, depth), jnp.float32),
        ],
        axis=0,
    )
    terms[...] = stack(*three_terms(rows), jnp.zeros_like(rows)).astype(jnp.bfloat16)
    factors = surface_factors(surface)
    for start in range(0, depth, LANES):
        cut = slice(start, start + LANES)
        anchors[cut] = factors[:, cut].T.astype(jnp.bfloat16)

    def lent_of(values, slot):
        index = jnp.broadcast_to(nodes[slot][3:4], (ROWS, LANES)).astype(jnp.int32)
        return pick(values, index)

    pair = 2 if parts % 2 == 0 else 1
    pairs = parts // pair
    turn = 1 - 2 * jnp.minimum((me // pair) // max(pairs // 2, 1), 1)

    def sums(step, _):
        base = lax.rem(me // pair + turn * step + pairs, pairs) * pair
        for k in range(pair):

            @pl.when(base + k != me)
            def _():
                pltpu.make_async_copy(
                    nodes.at[base + k], nodes.at[base + k], node_recv_sems.at[base + k]
                ).wait()

        places = jnp.concatenate(
            [node_factors(nodes[base + k]) for k in range(pair)], axis=1
        ).astype(jnp.bfloat16)
        total = jnp.zeros((4 * ROWS, pair * LANES), jnp.float32)
        for start in range(0, depth, CHUNK):
            for row in range(start, start + CHUNK, STEP):
                cut = slice(row, row + STEP)
                spread = jnp.dot(anchors[cut], places, preferred_element_type=jnp.float32)
                root = lax.rsqrt(spread)
                weight = root * root * root
                top = weight.astype(jnp.bfloat16)
                high[cut] = top
                low[cut] = (weight - top.astype(jnp.float32)).astype(jnp.bfloat16)
            cut = slice(start, start + CHUNK)
            left = terms[:, cut]
            total = total + jnp.dot(left, high[cut], preferred_element_type=jnp.float32)
            total = total + jnp.dot(left, low[cut], preferred_element_type=jnp.float32)
        added = total[0:ROWS] + total[ROWS : 2 * ROWS] + total[2 * ROWS : 3 * ROWS]
        halves = [added[:, k * LANES : (k + 1) * LANES] for k in range(pair)]
        for k in range(pair):
            partial[base + k] = halves[k]
        for k in range(pair):
            lent[base + k] = lent_of(halves[k], base + k)
        for k in range(pair):
            block = base + k
            is_mine = block == me

            @pl.when(is_mine)
            def _():
                got_own[me] = halves[k]

            @pl.when(jnp.logical_not(is_mine))
            def _():
                remote(
                    partial.at[block], got_own.at[me], send_sems.at[0], recv_sems.at[0], (tile, block)
                ).start()

            is_end = block == parts - 1
            owner = (jnp.where(is_end, after, tile), jnp.where(is_end, 0, block + 1))

            @pl.when(block + 1 == me)
            def _():
                got_before[me] = lent[block]

            @pl.when(block + 1 != me)
            def _():
                remote(
                    lent.at[block], got_before.at[me], send_sems.at[1], recv_sems.at[1], owner
                ).start()

            is_start = block == 0
            other = (jnp.where(is_start, before, tile), jnp.where(is_start, parts - 1, block - 1))

            @pl.when(block - 1 == me)
            def _():
                got_after[me] = lent[block]

            @pl.when(block - 1 != me)
            def _():
                remote(
                    lent.at[block], got_after.at[me], send_sems.at[2], recv_sems.at[2], other
                ).start()

        return 0

    lax.fori_loop(0, pairs, sums, 0)

    loads[5].wait()
    groups = cells_ref.shape[1] // LANES
    corner = jnp.concatenate(
        [
            cells_ref[k : k + 1, g * LANES : (g + 1) * LANES]
            for k in range(4)
            for g in range(groups)
        ],
        axis=0,
    )
    is_own = (corner >= width) & (corner < width + LANES)
    own_at = jnp.where(is_own, corner - width, 0)
    lent_at = jnp.where(is_own, 0, jnp.where(corner < width, corner, corner - LANES))

    def corners(own_row, lent_row):
        found = []
        for r in range(0, 4 * groups, ROWS):
            cut = slice(r, r + ROWS)
            found.append(
                jnp.where(
                    is_own[cut],
                    pick(jnp.broadcast_to(own_row, (ROWS, LANES)), own_at[cut]),
                    pick(jnp.broadcast_to(lent_row, (ROWS, LANES)), lent_at[cut]),
                )
            )
        whole = jnp.concatenate(found, axis=0)
        return [whole[k * groups : (k + 1) * groups] for k in range(4)]

    lane = lax.broadcasted_iota(jnp.int32, (ROWS, LANES), 1)
    is_before = lane < width

    @pl.when(is_first)
    def _():
        pltpu.make_async_copy(nodes.at[parts], nodes.at[parts], node_recv_sems.at[parts]).wait()

    @pl.when(is_last)
    def _():
        pltpu.make_async_copy(
            nodes.at[parts + 1], nodes.at[parts + 1], node_recv_sems.at[parts + 1]
        ).wait()

    slot_before = jnp.where(is_first, parts, me - 1)
    slot_after = jnp.where(is_last, parts + 1, me + 1)
    lent_nodes = jnp.where(
        is_before,
        lent_of(nodes[slot_before], slot_before),
        lent_of(nodes[slot_after], slot_after),
    )
    place = [corners(mine[k : k + 1], lent_nodes[k : k + 1]) for k in range(3)]

    bulk(got_own, parts - 1, recv_sems.at[0]).wait()
    own_totals = jnp.sum(got_own[...], axis=0)
    own_motion = node_shift(own_totals, mine)
    motion_ref[...] = jnp.concatenate(own_motion, axis=0)
    save_motion = pltpu.make_async_copy(motion_ref, motion_out, load_sems.at[6])
    save_motion.start()

    def wait_side(ref, is_edge, sem):
        @pl.when(is_edge)
        def _():
            bulk(ref, parts, sem).wait()

        @pl.when(jnp.logical_not(is_edge))
        def _():
            bulk(ref, parts - 1, sem).wait()

    wait_side(got_before, is_first, recv_sems.at[1])
    wait_side(got_after, is_last, recv_sems.at[2])
    lent_totals = jnp.where(
        is_before, jnp.sum(got_before[...], axis=0), jnp.sum(got_after[...], axis=0)
    )
    lent_motion = node_shift(lent_totals, lent_nodes)
    shift = [corners(own_motion[k], lent_motion[k]) for k in range(3)]

    half = [[place[k][c] + 0.5 * shift[k][c] for c in range(4)] for k in range(3)]
    swept = jnp.zeros((groups, LANES), jnp.float32)
    for first, second, third in FACES:
        normal = cross(
            [half[k][second] - half[k][first] for k in range(3)],
            [half[k][third] - half[k][first] for k in range(3)],
        )
        for k in range(3):
            swept = swept + (shift[k][first] + shift[k][second] + shift[k][third]) * normal[k]
    swept_ref[...] = swept * (1.0 / 6.0)
    save_swept = pltpu.make_async_copy(swept_ref, swept_out, load_sems.at[7])
    save_swept.start()

    bulk(nodes, parts - 1, node_send_sems.at[0]).wait()

    @pl.when(is_first)
    def _():
        bulk(nodes, 1, node_send_sems.at[1]).wait()

    @pl.when(is_last)
    def _():
        bulk(nodes, 1, node_send_sems.at[1]).wait()

    bulk(partial, parts - 1, send_sems.at[0]).wait()
    wait_side(lent, is_first, send_sems.at[1])
    wait_side(lent, is_last, send_sems.at[2])
    save_motion.wait()
    save_swept.wait()


def hand_on(motion_in, swept_in, motion_out, swept_out, sems):
    copies = [
        pltpu.make_async_copy(motion_in, motion_out, sems.at[0]),
        pltpu.make_async_copy(swept_in, swept_out, sems.at[1]),
    ]
    for copy in copies:
        copy.start()
    for copy in copies:
        copy.wait()


def shards(tiles, parts, points, surface_points, displacement, rotation, halo_index, connectivity):
    width = halo_index.shape[0]
    depth = surface_points.shape[1]
    cells = connectivity.shape[1]
    groups = cells // LANES
    pair = 2 if parts % 2 == 0 else 1
    block = (ROWS, LANES)
    dma = pltpu.SemaphoreType.DMA
    outputs = (
        jax.ShapeDtypeStruct((3, LANES), jnp.float32),
        jax.ShapeDtypeStruct((groups, LANES), jnp.float32),
    )
    motion, swept = pl.pallas_call(
        functools.partial(kernel, tiles, parts, width),
        out_shape=outputs,
        in_specs=[pl.BlockSpec(memory_space=pltpu.HBM)] * 6,
        out_specs=(pl.BlockSpec(memory_space=pl.ANY),) * 2,
        scratch_shapes=[
            pltpu.VMEM((3, LANES), jnp.float32),
            pltpu.VMEM((3, depth), jnp.float32),
            pltpu.VMEM((3, depth), jnp.float32),
            pltpu.VMEM((3, depth), jnp.float32),
            pltpu.VMEM((1, width), jnp.int32),
            pltpu.VMEM((4, cells), jnp.int32),
            pltpu.VMEM((parts + 2, *block), jnp.float32),
            pltpu.VMEM((depth, 6 * ROWS), jnp.bfloat16),
            pltpu.VMEM((4 * ROWS, depth), jnp.bfloat16),
            pltpu.VMEM((depth, pair * LANES), jnp.bfloat16),
            pltpu.VMEM((depth, pair * LANES), jnp.bfloat16),
            pltpu.VMEM((parts, *block), jnp.float32),
            pltpu.VMEM((parts, *block), jnp.float32),
            pltpu.VMEM((parts, *block), jnp.float32),
            pltpu.VMEM((parts, *block), jnp.float32),
            pltpu.VMEM((parts, *block), jnp.float32),
            pltpu.VMEM((3, LANES), jnp.float32),
            pltpu.VMEM((groups, LANES), jnp.float32),
            dma((8,)),
            dma((2,)),
            dma((parts + 2,)),
            dma((3,)),
            dma((3,)),
        ],
        compiler_params=pltpu.CompilerParams(
            collective_id=0, has_side_effects=True, vmem_limit_bytes=60 * 1024 * 1024
        ),
        cost_estimate=pl.CostEstimate(
            flops=2 * 7 * parts * LANES * depth,
            bytes_accessed=4 * (9 * depth + 4 * cells),
            transcendentals=parts * LANES * depth,
        ),
    )(points, surface_points, displacement, rotation, halo_index.reshape(1, width), connectivity)
    motion, swept = pl.pallas_call(
        hand_on,
        out_shape=outputs,
        in_specs=[pl.BlockSpec(memory_space=pl.ANY)] * 2,
        out_specs=(pl.BlockSpec(memory_space=pl.ANY),) * 2,
        scratch_shapes=[dma((2,))],
        compiler_params=pltpu.CompilerParams(vmem_limit_bytes=60 * 1024 * 1024),
    )(motion, swept)
    return motion, swept.reshape(cells)


def solution(mesh):
    in_specs = (
        P(None, ("vol", "surf")),
        P(None, "surf"),
        P(None, "surf"),
        P(None, "surf"),
        P(("vol", "surf")),
        P(None, ("vol", "surf")),
    )
    out_specs = (P(None, ("vol", "surf")), P(("vol", "surf")))
    body = functools.partial(shards, mesh.shape["vol"], mesh.shape["surf"])
    return jax.shard_map(body, mesh=mesh, in_specs=in_specs, out_specs=out_specs, check_vma=False)
```

```python
import functools

import jax
import jax.numpy as jnp
from jax import lax
from jax.experimental import pallas as pl
from jax.experimental.pallas import tpu as pltpu
from jax.sharding import PartitionSpec as P

SOFTENING = 0.01
LANES = 128
ROWS = 8
CHUNK = 256
STEP = 64
FACES = ((1, 2, 3), (0, 3, 2), (0, 1, 3), (0, 2, 1))
MESH = pl.DeviceIdType.MESH


def cross(a, b):
    return (
        a[1] * b[2] - a[2] * b[1],
        a[2] * b[0] - a[0] * b[2],
        a[0] * b[1] - a[1] * b[0],
    )


def three_terms(rows):
    first = rows.astype(jnp.bfloat16).astype(jnp.float32)
    rest = rows - first
    second = rest.astype(jnp.bfloat16).astype(jnp.float32)
    return first, second, (rest - second).astype(jnp.bfloat16).astype(jnp.float32)


def stack(*blocks):
    return jnp.concatenate(blocks, axis=0)


def node_factors(rows):
    x, y, z = rows[0:1], rows[1:2], rows[2:3]
    ones = jnp.ones_like(x)
    first, second, third = three_terms(
        stack(-2.0 * x, -2.0 * y, -2.0 * z, x * x + y * y + z * z, ones, 0.0 * ones, 0.0 * ones, 0.0 * ones)
    )
    return stack(first, first, second, second, first, third)


def surface_factors(rows):
    x, y, z = rows[0:1], rows[1:2], rows[2:3]
    ones = jnp.ones_like(x)
    first, second, third = three_terms(
        stack(x, y, z, ones, x * x + y * y + (z * z + SOFTENING), 0.0 * ones, 0.0 * ones, 0.0 * ones)
    )
    return stack(first, second, first, second, third, first)


def pick(rows, index):
    return jnp.take_along_axis(rows, index, axis=1)


def node_shift(totals, rows):
    turn = cross((totals[3:4], totals[4:5], totals[5:6]), (rows[0:1], rows[1:2], rows[2:3]))
    scale = 1.0 / totals[6:7]
    return tuple((totals[k : k + 1] + turn[k]) * scale for k in range(3))


def kernel(
    tiles,
    parts,
    width,
    points_in,
    surface_in,
    displacement_in,
    rotation_in,
    halo_in,
    cells_in,
    motion_ref,
    swept_ref,
    points_ref,
    surface_ref,
    displacement_ref,
    rotation_ref,
    halo_ref,
    cells_ref,
    nodes,
    anchors,
    terms,
    high,
    low,
    staged,
    got_pair,
    got_side,
    load_sems,
    node_send_sems,
    node_recv_sems,
    send_sems,
    recv_sems,
):
    tile = lax.axis_index("vol")
    me = lax.axis_index("surf")
    before = lax.rem(tile + tiles - 1, tiles)
    after = lax.rem(tile + 1, tiles)
    is_first = me == 0
    is_last = me == parts - 1

    sources = (points_in, halo_in, surface_in, rotation_in, displacement_in, cells_in)
    targets = (points_ref, halo_ref, surface_ref, rotation_ref, displacement_ref, cells_ref)
    loads = [
        pltpu.make_async_copy(source, target, load_sems.at[k])
        for k, (source, target) in enumerate(zip(sources, targets))
    ]
    for load in loads:
        load.start()

    def bulk(ref, count, sem):
        return pltpu.make_async_copy(ref.at[pl.ds(0, count)], ref.at[pl.ds(0, count)], sem)

    def remote(src, dst, send_sem, recv_sem, device):
        return pltpu.make_async_remote_copy(
            src_ref=src,
            dst_ref=dst,
            send_sem=send_sem,
            recv_sem=recv_sem,
            device_id=device,
            device_id_type=MESH,
        )

    barrier = pltpu.get_barrier_semaphore()

    def greet(step, _):
        other = lax.rem(me + step, parts)
        pl.semaphore_signal(barrier, inc=1, device_id=(tile, other), device_id_type=MESH)
        return 0

    def greet_far(far):
        def body(other, _):
            pl.semaphore_signal(barrier, inc=1, device_id=(far, other), device_id_type=MESH)
            return 0

        lax.fori_loop(0, parts, body, 0)

    lax.fori_loop(1, parts, greet, 0)

    @pl.when(is_first)
    def _():
        greet_far(before)

    @pl.when(is_last)
    def _():
        greet_far(after)

    loads[0].wait()
    loads[1].wait()
    halo = halo_ref[...].astype(jnp.float32)
    halo_row = jnp.concatenate([halo] * (LANES // width), axis=1)
    mine = jnp.concatenate(
        [points_ref[...], halo_row, jnp.zeros((ROWS - 4, LANES), jnp.float32)], axis=0
    )
    nodes[me] = mine
    for load in loads[2:5]:
        load.wait()
    depth = surface_ref.shape[1]
    surface = surface_ref[...]
    rotation = rotation_ref[...]
    turned = cross(
        tuple(rotation[k : k + 1] for k in range(3)), tuple(surface[k : k + 1] for k in range(3))
    )
    rows = jnp.concatenate(
        [
            displacement_ref[...] - jnp.concatenate(turned, axis=0),
            rotation,
            jnp.ones((1, depth), jnp.float32),
            jnp.zeros((1, depth), jnp.float32),
        ],
        axis=0,
    )
    terms[...] = stack(*three_terms(rows), jnp.zeros_like(rows)).astype(jnp.bfloat16)
    factors = surface_factors(surface)
    for start in range(0, depth, LANES):
        cut = slice(start, start + LANES)
        anchors[cut] = factors[:, cut].T.astype(jnp.bfloat16)

    pl.semaphore_wait(barrier, parts + 1)

    def share(step, _):
        other = lax.rem(me + step, parts)
        remote(
            nodes.at[me], nodes.at[me], node_send_sems.at[0], node_recv_sems.at[me], (tile, other)
        ).start()
        return 0

    lax.fori_loop(1, parts, share, 0)

    def share_far(slot, device):
        remote(
            nodes.at[me], nodes.at[slot], node_send_sems.at[1], node_recv_sems.at[slot], device
        ).start()

    @pl.when(is_last)
    def _():
        share_far(parts, (after, 0))

    @pl.when(is_first)
    def _():
        share_far(parts + 1, (before, parts - 1))

    def lent_of(values, slot):
        index = jnp.broadcast_to(nodes[slot][3:4], (ROWS, LANES)).astype(jnp.int32)
        return pick(values, index)

    pair = 2
    pairs = parts // pair
    turn = 1 - 2 * jnp.minimum((me // pair) // max(pairs // 2, 1), 1)

    def sums(step, _):
        base = lax.rem(me // pair + turn * step + pairs, pairs) * pair
        for k in range(pair):

            @pl.when(base + k != me)
            def _():
                pltpu.make_async_copy(
                    nodes.at[base + k], nodes.at[base + k], node_recv_sems.at[base + k]
                ).wait()

        places = jnp.concatenate(
            [node_factors(nodes[base + k]) for k in range(pair)], axis=1
        ).astype(jnp.bfloat16)
        total = jnp.zeros((4 * ROWS, pair * LANES), jnp.float32)
        for start in range(0, depth, CHUNK):
            for row in range(start, start + CHUNK, STEP):
                cut = slice(row, row + STEP)
                spread = jnp.dot(anchors[cut], places, preferred_element_type=jnp.float32)
                root = lax.rsqrt(spread)
                weight = root * root * root
                top = weight.astype(jnp.bfloat16)
                high[cut] = top
                low[cut] = (weight - top.astype(jnp.float32)).astype(jnp.bfloat16)
            cut = slice(start, start + CHUNK)
            left = terms[:, cut]
            total = total + jnp.dot(left, high[cut], preferred_element_type=jnp.float32)
            total = total + jnp.dot(left, low[cut], preferred_element_type=jnp.float32)
        added = total[0:ROWS] + total[ROWS : 2 * ROWS] + total[2 * ROWS : 3 * ROWS]
        halves = [added[:, 0:LANES], added[:, LANES:]]
        for k in range(2):
            staged[base + k, 0] = halves[k]
            staged[base + 1 - k, 1] = lent_of(halves[k], base + k)
        for k in range(2):
            block = base + k

            @pl.when(block != me)
            def _():
                remote(
                    staged.at[block], got_pair.at[me], send_sems.at[0], recv_sems.at[0], (tile, block)
                ).start()

        is_start = base == 0
        is_end = base == parts - 2
        sides = (
            (1, base - 1, jnp.where(is_start, before, tile), jnp.where(is_start, parts - 1, base - 1)),
            (0, base + 2, jnp.where(is_end, after, tile), jnp.where(is_end, 0, base + 2)),
        )
        for k, block, owner_tile, owner in sides:

            @pl.when(block != me)
            def _():
                remote(
                    staged.at[base + k, 1],
                    got_side.at[me],
                    send_sems.at[1],
                    recv_sems.at[1],
                    (owner_tile, owner),
                ).start()

        return 0

    lax.fori_loop(0, pairs, sums, 0)
    got_pair[me] = staged[me]
    is_odd = lax.rem(me, 2)
    is_edge = is_first | is_last

    @pl.when(jnp.logical_not(is_edge))
    def _():
        got_side[me] = staged[me - 2 + 4 * is_odd, 1]

    loads[5].wait()
    groups = cells_ref.shape[1] // LANES
    corner = jnp.concatenate(
        [
            cells_ref[k : k + 1, g * LANES : (g + 1) * LANES]
            for k in range(4)
            for g in range(groups)
        ],
        axis=0,
    )
    is_own = (corner >= width) & (corner < width + LANES)
    own_at = jnp.where(is_own, corner - width, 0)
    lent_at = jnp.where(is_own, 0, jnp.where(corner < width, corner, corner - LANES))

    def corners(own_row, lent_row):
        found = []
        for r in range(0, 4 * groups, ROWS):
            cut = slice(r, r + ROWS)
            found.append(
                jnp.where(
                    is_own[cut],
                    pick(jnp.broadcast_to(own_row, (ROWS, LANES)), own_at[cut]),
                    pick(jnp.broadcast_to(lent_row, (ROWS, LANES)), lent_at[cut]),
                )
            )
        whole = jnp.concatenate(found, axis=0)
        return [whole[k * groups : (k + 1) * groups] for k in range(4)]

    lane = lax.broadcasted_iota(jnp.int32, (ROWS, LANES), 1)
    is_before = lane < width

    @pl.when(is_first)
    def _():
        pltpu.make_async_copy(nodes.at[parts], nodes.at[parts], node_recv_sems.at[parts]).wait()

    @pl.when(is_last)
    def _():
        pltpu.make_async_copy(
            nodes.at[parts + 1], nodes.at[parts + 1], node_recv_sems.at[parts + 1]
        ).wait()

    slot_before = jnp.where(is_first, parts, me - 1)
    slot_after = jnp.where(is_last, parts + 1, me + 1)
    lent_nodes = jnp.where(
        is_before,
        lent_of(nodes[slot_before], slot_before),
        lent_of(nodes[slot_after], slot_after),
    )
    place = [corners(mine[k : k + 1], lent_nodes[k : k + 1]) for k in range(3)]

    bulk(got_pair, parts - 1, recv_sems.at[0]).wait()
    own_totals = jnp.sum(got_pair[:, 0], axis=0)
    near_totals = jnp.sum(got_pair[:, 1], axis=0)
    own_motion = node_shift(own_totals, mine)
    motion_ref[...] = jnp.concatenate(own_motion, axis=0)

    def wait_side(ref, sem):
        @pl.when(is_edge)
        def _():
            bulk(ref, parts, sem).wait()

        @pl.when(jnp.logical_not(is_edge))
        def _():
            bulk(ref, parts - 1, sem).wait()

    wait_side(got_side, recv_sems.at[1])
    side_totals = jnp.sum(got_side[...], axis=0)
    from_near = (lane >= width) == (jnp.broadcast_to(is_odd, (ROWS, LANES)) == 0)
    lent_totals = jnp.where(from_near, near_totals, side_totals)
    lent_motion = node_shift(lent_totals, lent_nodes)
    shift = [corners(own_motion[k], lent_motion[k]) for k in range(3)]

    half = [[place[k][c] + 0.5 * shift[k][c] for c in range(4)] for k in range(3)]
    swept = jnp.zeros((groups, LANES), jnp.float32)
    for first, second, third in FACES:
        normal = cross(
            [half[k][second] - half[k][first] for k in range(3)],
            [half[k][third] - half[k][first] for k in range(3)],
        )
        for k in range(3):
            swept = swept + (shift[k][first] + shift[k][second] + shift[k][third]) * normal[k]
    swept_ref[...] = swept * (1.0 / 6.0)

    bulk(nodes, parts - 1, node_send_sems.at[0]).wait()

    @pl.when(is_first)
    def _():
        bulk(nodes, 1, node_send_sems.at[1]).wait()

    @pl.when(is_last)
    def _():
        bulk(nodes, 1, node_send_sems.at[1]).wait()

    bulk(staged, parts - 1, send_sems.at[0]).wait()
    wait_side(got_side, send_sems.at[1])


def hand_on(motion_in, swept_in, motion_out, swept_out, sems):
    copies = [
        pltpu.make_async_copy(motion_in, motion_out, sems.at[0]),
        pltpu.make_async_copy(swept_in, swept_out, sems.at[1]),
    ]
    for copy in copies:
        copy.start()
    for copy in copies:
        copy.wait()


def shards(tiles, parts, points, surface_points, displacement, rotation, halo_index, connectivity):
    width = halo_index.shape[0]
    depth = surface_points.shape[1]
    cells = connectivity.shape[1]
    groups = cells // LANES
    pair = 2
    block = (ROWS, LANES)
    dma = pltpu.SemaphoreType.DMA
    inputs = (
        points,
        surface_points,
        displacement,
        rotation,
        halo_index.reshape(1, width),
        connectivity,
    )
    outputs = (
        jax.ShapeDtypeStruct((3, LANES), jnp.float32),
        jax.ShapeDtypeStruct((groups, LANES), jnp.float32),
    )
    motion, swept = pl.pallas_call(
        functools.partial(kernel, tiles, parts, width),
        out_shape=outputs,
        in_specs=[pl.BlockSpec(memory_space=pltpu.HBM)] * 6,
        out_specs=(pl.BlockSpec(memory_space=pltpu.VMEM),) * 2,
        scratch_shapes=[
            pltpu.VMEM((3, LANES), jnp.float32),
            pltpu.VMEM((3, depth), jnp.float32),
            pltpu.VMEM((3, depth), jnp.float32),
            pltpu.VMEM((3, depth), jnp.float32),
            pltpu.VMEM((1, width), jnp.int32),
            pltpu.VMEM((4, cells), jnp.int32),
            pltpu.VMEM((parts + 2, *block), jnp.float32),
            pltpu.VMEM((depth, 6 * ROWS), jnp.bfloat16),
            pltpu.VMEM((4 * ROWS, depth), jnp.bfloat16),
            pltpu.VMEM((depth, pair * LANES), jnp.bfloat16),
            pltpu.VMEM((depth, pair * LANES), jnp.bfloat16),
            pltpu.VMEM((parts, 2, *block), jnp.float32),
            pltpu.VMEM((parts, 2, *block), jnp.float32),
            pltpu.VMEM((parts, *block), jnp.float32),
            dma((6,)),
            dma((2,)),
            dma((parts + 2,)),
            dma((2,)),
            dma((2,)),
        ],
        compiler_params=pltpu.CompilerParams(
            collective_id=0, has_side_effects=True, vmem_limit_bytes=16 * 1024 * 1024
        ),
        cost_estimate=pl.CostEstimate(
            flops=2 * 7 * parts * LANES * depth,
            bytes_accessed=4 * (9 * depth + 4 * cells),
            transcendentals=parts * LANES * depth,
        ),
    )(*(pltpu.with_memory_space_constraint(array, pltpu.HBM) for array in inputs))
    motion, swept = pl.pallas_call(
        hand_on,
        out_shape=outputs,
        in_specs=[pl.BlockSpec(memory_space=pltpu.VMEM)] * 2,
        out_specs=(pl.BlockSpec(memory_space=pl.ANY),) * 2,
        scratch_shapes=[dma((2,))],
    )(motion, swept)
    return motion, swept.reshape(cells)


def solution(mesh):
    in_specs = (
        P(None, ("vol", "surf")),
        P(None, "surf"),
        P(None, "surf"),
        P(None, "surf"),
        P(("vol", "surf")),
        P(None, ("vol", "surf")),
    )
    out_specs = (P(None, ("vol", "surf")), P(("vol", "surf")))
    body = functools.partial(shards, mesh.shape["vol"], mesh.shape["surf"])
    return jax.shard_map(body, mesh=mesh, in_specs=in_specs, out_specs=out_specs, check_vma=False)
```

```python
import functools

import jax
import jax.numpy as jnp
from jax import lax
from jax.experimental import pallas as pl
from jax.experimental.pallas import tpu as pltpu
from jax.sharding import PartitionSpec as P

SOFTENING = 0.01
LANES = 128
ROWS = 8
CHUNK = 256
STEP = 256
FACES = ((1, 2, 3), (0, 3, 2), (0, 1, 3), (0, 2, 1))
MESH = pl.DeviceIdType.MESH


def cross(a, b):
    return (
        a[1] * b[2] - a[2] * b[1],
        a[2] * b[0] - a[0] * b[2],
        a[0] * b[1] - a[1] * b[0],
    )


def three_terms(rows):
    first = rows.astype(jnp.bfloat16).astype(jnp.float32)
    rest = rows - first
    second = rest.astype(jnp.bfloat16).astype(jnp.float32)
    return first, second, (rest - second).astype(jnp.bfloat16).astype(jnp.float32)


def stack(*blocks):
    return jnp.concatenate(blocks, axis=0)


def node_factors(rows):
    x, y, z = rows[0:1], rows[1:2], rows[2:3]
    ones = jnp.ones_like(x)
    first, second, third = three_terms(
        stack(-2.0 * x, -2.0 * y, -2.0 * z, x * x + y * y + z * z, ones, 0.0 * ones, 0.0 * ones, 0.0 * ones)
    )
    return stack(first, first, second, second, first, third)


def surface_factors(rows):
    x, y, z = rows[0:1], rows[1:2], rows[2:3]
    ones = jnp.ones_like(x)
    first, second, third = three_terms(
        stack(x, y, z, ones, x * x + y * y + (z * z + SOFTENING), 0.0 * ones, 0.0 * ones, 0.0 * ones)
    )
    return stack(first, second, first, second, third, first)


def pick(rows, index):
    return jnp.take_along_axis(rows, index, axis=1)


def node_shift(totals, rows):
    turn = cross((totals[3:4], totals[4:5], totals[5:6]), (rows[0:1], rows[1:2], rows[2:3]))
    scale = 1.0 / totals[6:7]
    return tuple((totals[k : k + 1] + turn[k]) * scale for k in range(3))


def kernel(
    tiles,
    parts,
    width,
    points_in,
    surface_in,
    displacement_in,
    rotation_in,
    halo_in,
    cells_in,
    motion_ref,
    swept_ref,
    points_ref,
    surface_ref,
    displacement_ref,
    rotation_ref,
    halo_ref,
    cells_ref,
    nodes,
    anchors,
    terms,
    high,
    low,
    staged,
    got_pair,
    got_side,
    load_sems,
    node_send_sems,
    node_recv_sems,
    send_sems,
    recv_sems,
):
    tile = lax.axis_index("vol")
    me = lax.axis_index("surf")
    before = lax.rem(tile + tiles - 1, tiles)
    after = lax.rem(tile + 1, tiles)
    is_first = me == 0
    is_last = me == parts - 1

    sources = (points_in, halo_in, surface_in, rotation_in, displacement_in, cells_in)
    targets = (points_ref, halo_ref, surface_ref, rotation_ref, displacement_ref, cells_ref)
    loads = [
        pltpu.make_async_copy(source, target, load_sems.at[k])
        for k, (source, target) in enumerate(zip(sources, targets))
    ]
    for load in loads:
        load.start()

    def bulk(ref, count, sem):
        return pltpu.make_async_copy(ref.at[pl.ds(0, count)], ref.at[pl.ds(0, count)], sem)

    def remote(src, dst, send_sem, recv_sem, device):
        return pltpu.make_async_remote_copy(
            src_ref=src,
            dst_ref=dst,
            send_sem=send_sem,
            recv_sem=recv_sem,
            device_id=device,
            device_id_type=MESH,
        )

    barrier = pltpu.get_barrier_semaphore()

    def greet(step, _):
        other = lax.rem(me + step, parts)
        pl.semaphore_signal(barrier, inc=1, device_id=(tile, other), device_id_type=MESH)
        return 0

    def greet_far(far):
        def body(other, _):
            pl.semaphore_signal(barrier, inc=1, device_id=(far, other), device_id_type=MESH)
            return 0

        lax.fori_loop(0, parts, body, 0)

    lax.fori_loop(1, parts, greet, 0)

    @pl.when(is_first)
    def _():
        greet_far(before)

    @pl.when(is_last)
    def _():
        greet_far(after)

    loads[0].wait()
    loads[1].wait()
    halo = halo_ref[...].astype(jnp.float32)
    halo_row = jnp.concatenate([halo] * (LANES // width), axis=1)
    mine = jnp.concatenate(
        [points_ref[...], halo_row, jnp.zeros((ROWS - 4, LANES), jnp.float32)], axis=0
    )
    nodes[me] = mine
    for load in loads[2:5]:
        load.wait()
    depth = surface_ref.shape[1]
    surface = surface_ref[...]
    rotation = rotation_ref[...]
    turned = cross(
        tuple(rotation[k : k + 1] for k in range(3)), tuple(surface[k : k + 1] for k in range(3))
    )
    rows = jnp.concatenate(
        [
            displacement_ref[...] - jnp.concatenate(turned, axis=0),
            rotation,
            jnp.ones((1, depth), jnp.float32),
            jnp.zeros((1, depth), jnp.float32),
        ],
        axis=0,
    )
    terms[...] = stack(*three_terms(rows), jnp.zeros_like(rows)).astype(jnp.bfloat16)
    factors = surface_factors(surface)
    for start in range(0, depth, LANES):
        cut = slice(start, start + LANES)
        anchors[cut] = factors[:, cut].T.astype(jnp.bfloat16)

    pl.semaphore_wait(barrier, parts + 1)

    def share(step, _):
        other = lax.rem(me + step, parts)
        remote(
            nodes.at[me], nodes.at[me], node_send_sems.at[0], node_recv_sems.at[me], (tile, other)
        ).start()
        return 0

    lax.fori_loop(1, parts, share, 0)

    def share_far(slot, device):
        remote(
            nodes.at[me], nodes.at[slot], node_send_sems.at[1], node_recv_sems.at[slot], device
        ).start()

    @pl.when(is_last)
    def _():
        share_far(parts, (after, 0))

    @pl.when(is_first)
    def _():
        share_far(parts + 1, (before, parts - 1))

    def lent_of(values, slot):
        index = jnp.broadcast_to(nodes[slot][3:4], (ROWS, LANES)).astype(jnp.int32)
        return pick(values, index)

    pair = 2
    pairs = parts // pair
    turn = 1 - 2 * jnp.minimum((me // pair) // max(pairs // 2, 1), 1)

    def sums(step, _):
        base = lax.rem(me // pair + turn * step + pairs, pairs) * pair
        for k in range(pair):

            @pl.when(base + k != me)
            def _():
                pltpu.make_async_copy(
                    nodes.at[base + k], nodes.at[base + k], node_recv_sems.at[base + k]
                ).wait()

        places = jnp.concatenate(
            [node_factors(nodes[base + k]) for k in range(pair)], axis=1
        ).astype(jnp.bfloat16)
        total = jnp.zeros((4 * ROWS, pair * LANES), jnp.float32)
        for start in range(0, depth, CHUNK):
            for row in range(start, start + CHUNK, STEP):
                cut = slice(row, row + STEP)
                spread = jnp.dot(anchors[cut], places, preferred_element_type=jnp.float32)
                root = lax.rsqrt(spread)
                weight = root * root * root
                top = weight.astype(jnp.bfloat16)
                high[cut] = top
                low[cut] = (weight - top.astype(jnp.float32)).astype(jnp.bfloat16)
            cut = slice(start, start + CHUNK)
            left = terms[:, cut]
            total = total + jnp.dot(left, high[cut], preferred_element_type=jnp.float32)
            total = total + jnp.dot(left, low[cut], preferred_element_type=jnp.float32)
        added = total[0:ROWS] + total[ROWS : 2 * ROWS] + total[2 * ROWS : 3 * ROWS]
        halves = [added[:, 0:LANES], added[:, LANES:]]
        for k in range(2):
            staged[base + k, 0] = halves[k]
            staged[base + 1 - k, 1] = lent_of(halves[k], base + k)
        for k in range(2):
            block = base + k

            @pl.when(block != me)
            def _():
                remote(
                    staged.at[block], got_pair.at[me], send_sems.at[0], recv_sems.at[0], (tile, block)
                ).start()

        is_start = base == 0
        is_end = base == parts - 2
        sides = (
            (1, base - 1, jnp.where(is_start, before, tile), jnp.where(is_start, parts - 1, base - 1)),
            (0, base + 2, jnp.where(is_end, after, tile), jnp.where(is_end, 0, base + 2)),
        )
        for k, block, owner_tile, owner in sides:

            @pl.when(block != me)
            def _():
                remote(
                    staged.at[base + k, 1],
                    got_side.at[me],
                    send_sems.at[1],
                    recv_sems.at[1],
                    (owner_tile, owner),
                ).start()

        return 0

    lax.fori_loop(0, pairs, sums, 0)
    got_pair[me] = staged[me]
    is_odd = lax.rem(me, 2)
    is_edge = is_first | is_last

    @pl.when(jnp.logical_not(is_edge))
    def _():
        got_side[me] = staged[me - 2 + 4 * is_odd, 1]

    loads[5].wait()
    groups = cells_ref.shape[1] // LANES
    corner = jnp.concatenate(
        [
            cells_ref[k : k + 1, g * LANES : (g + 1) * LANES]
            for k in range(4)
            for g in range(groups)
        ],
        axis=0,
    )
    is_own = (corner >= width) & (corner < width + LANES)
    own_at = jnp.where(is_own, corner - width, 0)
    lent_at = jnp.where(is_own, 0, jnp.where(corner < width, corner, corner - LANES))

    def corners(own_row, lent_row):
        found = []
        for r in range(0, 4 * groups, ROWS):
            cut = slice(r, r + ROWS)
            found.append(
                jnp.where(
                    is_own[cut],
                    pick(jnp.broadcast_to(own_row, (ROWS, LANES)), own_at[cut]),
                    pick(jnp.broadcast_to(lent_row, (ROWS, LANES)), lent_at[cut]),
                )
            )
        whole = jnp.concatenate(found, axis=0)
        return [whole[k * groups : (k + 1) * groups] for k in range(4)]

    lane = lax.broadcasted_iota(jnp.int32, (ROWS, LANES), 1)
    is_before = lane < width

    @pl.when(is_first)
    def _():
        pltpu.make_async_copy(nodes.at[parts], nodes.at[parts], node_recv_sems.at[parts]).wait()

    @pl.when(is_last)
    def _():
        pltpu.make_async_copy(
            nodes.at[parts + 1], nodes.at[parts + 1], node_recv_sems.at[parts + 1]
        ).wait()

    slot_before = jnp.where(is_first, parts, me - 1)
    slot_after = jnp.where(is_last, parts + 1, me + 1)
    lent_nodes = jnp.where(
        is_before,
        lent_of(nodes[slot_before], slot_before),
        lent_of(nodes[slot_after], slot_after),
    )
    place = [corners(mine[k : k + 1], lent_nodes[k : k + 1]) for k in range(3)]

    bulk(got_pair, parts - 1, recv_sems.at[0]).wait()
    own_totals = jnp.sum(got_pair[:, 0], axis=0)
    near_totals = jnp.sum(got_pair[:, 1], axis=0)
    own_motion = node_shift(own_totals, mine)
    motion_ref[...] = jnp.concatenate(own_motion, axis=0)

    def wait_side(ref, sem):
        @pl.when(is_edge)
        def _():
            bulk(ref, parts, sem).wait()

        @pl.when(jnp.logical_not(is_edge))
        def _():
            bulk(ref, parts - 1, sem).wait()

    wait_side(got_side, recv_sems.at[1])
    side_totals = jnp.sum(got_side[...], axis=0)
    from_near = (lane >= width) == (jnp.broadcast_to(is_odd, (ROWS, LANES)) == 0)
    lent_totals = jnp.where(from_near, near_totals, side_totals)
    lent_motion = node_shift(lent_totals, lent_nodes)
    shift = [corners(own_motion[k], lent_motion[k]) for k in range(3)]

    half = [[place[k][c] + 0.5 * shift[k][c] for c in range(4)] for k in range(3)]
    swept = jnp.zeros((groups, LANES), jnp.float32)
    for first, second, third in FACES:
        normal = cross(
            [half[k][second] - half[k][first] for k in range(3)],
            [half[k][third] - half[k][first] for k in range(3)],
        )
        for k in range(3):
            swept = swept + (shift[k][first] + shift[k][second] + shift[k][third]) * normal[k]
    swept_ref[...] = swept * (1.0 / 6.0)

    bulk(nodes, parts - 1, node_send_sems.at[0]).wait()

    @pl.when(is_first)
    def _():
        bulk(nodes, 1, node_send_sems.at[1]).wait()

    @pl.when(is_last)
    def _():
        bulk(nodes, 1, node_send_sems.at[1]).wait()

    bulk(staged, parts - 1, send_sems.at[0]).wait()
    wait_side(got_side, send_sems.at[1])


def hand_on(motion_in, swept_in, motion_out, swept_out, sems):
    copies = [
        pltpu.make_async_copy(motion_in, motion_out, sems.at[0]),
        pltpu.make_async_copy(swept_in, swept_out, sems.at[1]),
    ]
    for copy in copies:
        copy.start()
    for copy in copies:
        copy.wait()


def shards(tiles, parts, points, surface_points, displacement, rotation, halo_index, connectivity):
    width = halo_index.shape[0]
    depth = surface_points.shape[1]
    cells = connectivity.shape[1]
    groups = cells // LANES
    pair = 2
    block = (ROWS, LANES)
    dma = pltpu.SemaphoreType.DMA
    inputs = (
        points,
        surface_points,
        displacement,
        rotation,
        halo_index.reshape(1, width),
        connectivity,
    )
    outputs = (
        jax.ShapeDtypeStruct((3, LANES), jnp.float32),
        jax.ShapeDtypeStruct((groups, LANES), jnp.float32),
    )
    motion, swept = pl.pallas_call(
        functools.partial(kernel, tiles, parts, width),
        out_shape=outputs,
        in_specs=[pl.BlockSpec(memory_space=pltpu.HBM)] * 6,
        out_specs=(pl.BlockSpec(memory_space=pltpu.VMEM),) * 2,
        scratch_shapes=[
            pltpu.VMEM((3, LANES), jnp.float32),
            pltpu.VMEM((3, depth), jnp.float32),
            pltpu.VMEM((3, depth), jnp.float32),
            pltpu.VMEM((3, depth), jnp.float32),
            pltpu.VMEM((1, width), jnp.int32),
            pltpu.VMEM((4, cells), jnp.int32),
            pltpu.VMEM((parts + 2, *block), jnp.float32),
            pltpu.VMEM((depth, 6 * ROWS), jnp.bfloat16),
            pltpu.VMEM((4 * ROWS, depth), jnp.bfloat16),
            pltpu.VMEM((depth, pair * LANES), jnp.bfloat16),
            pltpu.VMEM((depth, pair * LANES), jnp.bfloat16),
            pltpu.VMEM((parts, 2, *block), jnp.float32),
            pltpu.VMEM((parts, 2, *block), jnp.float32),
            pltpu.VMEM((parts, *block), jnp.float32),
            dma((6,)),
            dma((2,)),
            dma((parts + 2,)),
            dma((2,)),
            dma((2,)),
        ],
        compiler_params=pltpu.CompilerParams(
            collective_id=0, has_side_effects=True, vmem_limit_bytes=16 * 1024 * 1024
        ),
        cost_estimate=pl.CostEstimate(
            flops=2 * 7 * parts * LANES * depth,
            bytes_accessed=4 * (9 * depth + 4 * cells),
            transcendentals=parts * LANES * depth,
        ),
    )(*(pltpu.with_memory_space_constraint(array, pltpu.HBM) for array in inputs))
    motion, swept = pl.pallas_call(
        hand_on,
        out_shape=outputs,
        in_specs=[pl.BlockSpec(memory_space=pltpu.VMEM)] * 2,
        out_specs=(pl.BlockSpec(memory_space=pl.ANY),) * 2,
        scratch_shapes=[dma((2,))],
        compiler_params=pltpu.CompilerParams(vmem_limit_bytes=1024 * 1024),
    )(motion, swept)
    return motion, swept.reshape(cells)


def solution(mesh):
    in_specs = (
        P(None, ("vol", "surf")),
        P(None, "surf"),
        P(None, "surf"),
        P(None, "surf"),
        P(("vol", "surf")),
        P(None, ("vol", "surf")),
    )
    out_specs = (P(None, ("vol", "surf")), P(("vol", "surf")))
    body = functools.partial(shards, mesh.shape["vol"], mesh.shape["surf"])
    return jax.shard_map(body, mesh=mesh, in_specs=in_specs, out_specs=out_specs, check_vma=False)
```
